512 devices in a mesh: dom: 64 (over z, y), rep: 8 (over x, core).
Axes of the slice: x: 4, y: 8, z: 8, core: 2. Of those that a mesh axis runs over, the one named last changes fastest.
Arguments:
- agg_feats: bfloat16 [65536, 256], P(('dom', 'rep')), may hold values from -6 to 6
- out_grad: bfloat16 [65536, 256], P(('dom', 'rep')), may hold values from -3 to 3
- w_in: bfloat16 [256, 256], replicated, may hold values from -0.375 to 0.375
- w_out: bfloat16 [256, 256], replicated, may hold values from -0.375 to 0.375
- bias_in: float32 [256], replicated, may hold values from -3 to 3
- self_weight: float32 [1], replicated, may hold values from 0 to 0.5
- mirror_rows: int32 [64, 8, 64, 32], P('dom', 'rep'), may hold values from 0 to 1023, as said below
- edge_src: int32 [64, 8, 4096], P('dom', 'rep'), may hold values from 0 to 3071, as said below
- edge_dst: int32 [64, 8, 4096], P('dom', 'rep'), may hold values from 0 to 3071
Outputs:
- grad_nodes: float32 [65536, 256], P(('dom', 'rep'))
- grad_w_in: float32 [256, 256], replicated
- grad_w_out: float32 [256, 256], replicated
- grad_bias: float32 [256], replicated
The draws below stay inside these ranges and needn't reach their ends.
Inputs may be any that keep to these rules, and one draw needn't show every extreme that they name: `mirror_rows`: for device (d, r) and group k the 32 rows are distinct and lie among the masters of device (k, r), rows r * 128 to (r + 1) * 128 - 1. `edge_src`: on each device exactly 256 edges have a source among the masters of each device of its group (rows q * 128 to (q + 1) * 128 - 1 for q below 8); the other half of the edges have a mirror slot as source.
All inputs are finite; a program needn't handle non-finite values.
Results may differ from the reference program's by a relative error of at most 0.008.
Values may be sent and summed in bfloat16 or wider, within the bound.
A program may use at most 64 MiB of HBM per device.

```python
import math
import jax
import jax.numpy as jnp
import numpy as np
from jax import lax

D = 256
H = 256
NODE_DEV = 128
EDGE_DEV = 4096
SLOT = 32
NODE_GRP = 1024
NODES = 65536
LOCAL = 3072
N_DOM = 64
N_REP = 8


def draw_mirror_rows(key, part):
    key = jax.random.fold_in(key, 11)
    key_base, key_step = jax.random.split(key)
    base = jax.random.randint(key_base, (N_DOM, N_REP, N_DOM, 1), 0, NODE_DEV)
    stride = 6 * jax.random.randint(key_step, (N_DOM, N_REP, N_DOM, 1), 0, max(NODE_DEV // 6, 1)) + 1
    positions = jnp.arange(SLOT, dtype=jnp.int32)[None, None, None, :]
    owner = jnp.arange(N_REP, dtype=jnp.int32)[None, :, None, None] * NODE_DEV
    return (owner + (base + positions * stride) % NODE_DEV).astype(jnp.int32)


def draw_edge_src(key, part):
    key = jax.random.fold_in(key, 12)
    key_perm, key_group, key_mirror = jax.random.split(key, 3)
    keys = jax.random.split(key_perm, N_DOM * N_REP)
    places = jax.vmap(lambda one: jax.random.permutation(one, EDGE_DEV))(keys).reshape(N_DOM, N_REP, EDGE_DEV)
    bucket = EDGE_DEV // (2 * N_REP)
    group_pick = jax.random.randint(key_group, (N_DOM, N_REP, EDGE_DEV), 0, NODE_DEV)
    mirror_pick = jax.random.randint(key_mirror, (N_DOM, N_REP, EDGE_DEV), 0, N_DOM * SLOT)
    owner = places // bucket
    group_rows = owner * NODE_DEV + group_pick
    mirror_rows = NODE_GRP + mirror_pick
    return jnp.where(places < N_REP * bucket, group_rows, mirror_rows).astype(jnp.int32)


def touch_ends(result, stream_key, smallest, top_value):
    longest = result.shape.index(max(result.shape))
    spots = []
    for shift in (0, 1):
        where = [jax.random.randint(jax.random.fold_in(stream_key, axis), (), 0, length) for axis, length in enumerate(result.shape)]
        where[longest] = (where[longest] + shift) % result.shape[longest]
        spots.append(tuple(where))
    return result.at[spots[0]].set(smallest).at[spots[1]].set(top_value)


def levels(stream_key, shape, cuts, smallest, high):
    gain, own = 1.0, jax.random.fold_in(stream_key, 6)
    for position, blocks in cuts:
        heights = jnp.exp(jax.random.uniform(jax.random.fold_in(own, position), (blocks,), jnp.float32, smallest / len(cuts), high / len(cuts)))
        gain = gain * jnp.repeat(heights, shape[position] // blocks).reshape([-1 if axis == position else 1 for axis in range(len(shape))])
    return gain


def rank_table(number_of, slope):
    portions = [(1 << 20) // math.isqrt(grade ** slope) + 1 for grade in range(1, number_of + 1)]
    scale = 1 + sum(portions) // (1 << 30)
    return np.cumsum(np.array([max(1, weight // scale) for weight in portions]))


def ranked(stream_key, shape, count, lean):
    table = rank_table(count, lean)
    lot = jax.random.randint(jax.random.fold_in(stream_key, 1), shape, 0, int(table[count - 1]))
    grade = jnp.searchsorted(jnp.asarray(table, jnp.int32), lot, side="right")
    return jax.random.permutation(jax.random.fold_in(stream_key, 2), count)[grade].astype(jnp.int32)


def normal_values(key, dims, scale, bound, cuts=(), kind=jnp.bfloat16):
    array = scale * jax.random.normal(key, dims, jnp.float32)
    if cuts:
        array = array * levels(key, dims, cuts, -0.22, 0.18)
    return jnp.clip(array, -bound, bound).astype(kind)


def setup_inputs(seed: int = 0) -> dict:
    seeds = jax.random.split(jax.random.key(seed), 10)
    agg_feats = normal_values(seeds[0], (NODES, D), 1.0, 6.0, ((0, 512),))
    out_grad = normal_values(seeds[1], (NODES, D), 0.5, 3.0, ((0, 512),))
    w_in = normal_values(seeds[2], (D, H), D ** -0.5, 0.375)
    w_out = normal_values(seeds[3], (H, D), H ** -0.5, 0.375)
    bias_in = normal_values(seeds[4], (H,), 0.5, 3.0, (), jnp.float32)
    self_weight = jnp.clip(jax.random.uniform(seeds[5], (1,), jnp.float32, 0.0, 0.5), 0.0, 0.5)
    mirror_rows = draw_mirror_rows(jax.random.fold_in(seeds[9], 71), 0)
    edge_src = draw_edge_src(jax.random.fold_in(seeds[9], 71), 0)
    edge_dst = touch_ends(ranked(seeds[8], (N_DOM, N_REP, EDGE_DEV), LOCAL, 2), jax.random.fold_in(seeds[8], 3), 0, LOCAL - 1).astype(jnp.int32)
    return {"agg_feats": agg_feats, "out_grad": out_grad, "w_in": w_in, "w_out": w_out, "bias_in": bias_in, "self_weight": self_weight, "mirror_rows": mirror_rows, "edge_src": edge_src, "edge_dst": edge_dst}


def reference(agg_feats, out_grad, w_in, w_out, bias_in, self_weight, mirror_rows, edge_src, edge_dst):
    preact = jnp.dot(agg_feats, w_in, preferred_element_type=jnp.float32) + bias_in
    gated = jax.nn.sigmoid(preact)
    activated = (preact * gated).astype(jnp.bfloat16)
    back_act = lax.dot_general(out_grad, w_out, (((1,), (1,)), ((), ())), preferred_element_type=jnp.float32)
    grad_pre = (back_act * gated * (1.0 + preact * (1.0 - gated))).astype(jnp.bfloat16)
    grad_agg = lax.dot_general(grad_pre, w_in, (((1,), (1,)), ((), ())), preferred_element_type=jnp.float32).astype(jnp.bfloat16)
    norm_scale = float(NODES) ** -0.5
    grad_w_out = lax.dot_general(activated, out_grad, (((0,), (0,)), ((), ())), preferred_element_type=jnp.float32) * norm_scale
    grad_w_in = lax.dot_general(agg_feats, grad_pre, (((0,), (0,)), ((), ())), preferred_element_type=jnp.float32) * norm_scale
    grad_bias = jnp.sum(grad_pre.astype(jnp.float32), axis=0) * norm_scale
    values = grad_agg.astype(jnp.float32)
    offsets = (jnp.arange(N_DOM, dtype=jnp.int32) * NODE_GRP)[:, None]

    def one_group(totals, domain):
        picked = lax.dynamic_index_in_dim(mirror_rows, domain, 0, keepdims=False)
        global_rows = (picked + offsets[None]).reshape(N_REP, N_DOM * SLOT)

        def to_global(local_rows):
            mirror_index = jnp.clip(local_rows - NODE_GRP, 0, N_DOM * SLOT - 1)
            mirrored = jnp.take_along_axis(global_rows, mirror_index, axis=1)
            return jnp.where(local_rows < NODE_GRP, domain * NODE_GRP + local_rows, mirrored)

        sources = to_global(lax.dynamic_index_in_dim(edge_src, domain, 0, keepdims=False)).reshape(-1)
        targets = to_global(lax.dynamic_index_in_dim(edge_dst, domain, 0, keepdims=False)).reshape(-1)
        totals = totals.at[sources].add(values[targets])
        return totals, None

    start = jnp.zeros((NODES, D), jnp.float32)
    totals, unused = lax.scan(one_group, start, jnp.arange(N_DOM, dtype=jnp.int32))
    grad_nodes = (1.0 + self_weight[0]) * values + totals
    return grad_nodes, grad_w_in, grad_w_out, grad_bias
```

```python
import functools

import jax
import jax.numpy as jnp
from jax import lax
from jax.experimental import pallas as pl
from jax.experimental.pallas import tpu as pltpu
from jax.sharding import PartitionSpec as P

MESH = pl.DeviceIdType.MESH
BF = jnp.bfloat16
F32 = jnp.float32

LINE = 8
ROWS = 128
SLOT = 32
HALF = 128
WIDE = 256
EDGES = 4096
ORDER = (0, 1, 7, 2, 6, 3, 5, 4)
FWD = ((0, 1), (7, 2), (6, 3), (5, 4))
BWD = ((0, 1), (7, 2), (6, 3), (5, 4))

STAGES = (
    "idx_a", "idx_b", "one_a", "one_b", "group", "w_rep", "b_rep", "w_z", "w_y", "w_zg", "w_repg",
    "back_a", "back_b", "gsum", "last_a", "last_b",
)
SEM = {name: i for i, name in enumerate(STAGES)}
TWO_A = len(STAGES)
TWO_B = TWO_A + len(FWD)
N_SEM = TWO_B + len(FWD)


def offset(i):
    odd = i % 2
    return (1 - odd) * ((i + 2) // 2) + odd * (LINE - (i + 1) // 2)


def times(count, step):
    def run(i, carry):
        step(i)
        return carry

    lax.fori_loop(0, count, run, 0)


def dot(a, b, dims=((1,), (0,))):
    return lax.dot_general(a, b, (dims, ((), ())), preferred_element_type=F32)


def kernel(
    agg_ref, og_ref, w_in_ref, w_out_ref, bias_ref, sw_ref, idx_a_ref, idx_b_ref, dst_ref, src_ref,
    nodes_ref, weights_ref, bsum_ref,
    ga_ref, grp, blk_a, blk_b, ia, ib, pt_a, pt_b, stage_a, stage_b, mir_a, mir_b,
    v_dst, v_src, wbuf, fetched, out_a, out_b, ra, rb, last_src_a, last_src_b, fa, fb, gout, gin,
    wsend, wrecv, bsend, brecv, zsend, zrecv, ysend, yrecv, zg, wfull, ssem, rsem,
):
    me = lax.axis_index("dom")
    r = lax.axis_index("rep")
    z, y = me // LINE, me % LINE

    def on_z(to):
        return (to * LINE + y, r)

    def on_y(to):
        return (z * LINE + to, r)

    def on_rep(to):
        return (me, to)

    def send(src, dst, sem, device):
        pltpu.make_async_remote_copy(
            src_ref=src, dst_ref=dst, send_sem=ssem.at[sem], recv_sem=rsem.at[sem],
            device_id=device, device_id_type=MESH,
        ).start()

    def got(view, sem):
        pltpu.make_async_copy(view, view, rsem.at[sem]).wait()

    def sent(view, sem):
        pltpu.make_async_copy(view, view, ssem.at[sem]).wait()

    barrier = pltpu.get_barrier_semaphore()

    def greet(i):
        for device in (on_z((z + i + 1) % LINE), on_y((y + i + 1) % LINE), on_rep((r + i + 1) % LINE)):
            pl.semaphore_signal(barrier, inc=1, device_id=device, device_id_type=MESH)

    times(LINE - 1, greet)

    agg, og = agg_ref[...], og_ref[...]
    preact = dot(agg, w_in_ref[...]) + bias_ref[...]
    gated = jax.nn.sigmoid(preact)
    back_act = dot(og, w_out_ref[...], ((1,), (1,)))
    grad_pre = (back_act * gated * (1.0 + preact * (1.0 - gated))).astype(BF)
    grad_agg = dot(grad_pre, w_in_ref[...], ((1,), (1,))).astype(BF)
    ga_ref[...] = grad_agg
    grp[r] = grad_agg
    blk_a[z] = grad_agg[:, :HALF]
    blk_b[y] = grad_agg[:, HALF:]
    ia[y] = idx_a_ref[y]
    ib[z] = idx_b_ref[z]

    pl.semaphore_wait(barrier, 3 * (LINE - 1))

    def send_idx(i):
        to = (y + offset(i)) % LINE
        send(idx_a_ref.at[to], ia.at[y], SEM["idx_a"], on_y(to))
        to = (z + offset(i)) % LINE
        send(idx_b_ref.at[to], ib.at[z], SEM["idx_b"], on_z(to))

    times(LINE - 1, send_idx)

    def send_blocks(i):
        send(blk_a.at[z], blk_a.at[z], SEM["one_a"], on_z((z + offset(i)) % LINE))
        send(blk_b.at[y], blk_b.at[y], SEM["one_b"], on_y((y + offset(i)) % LINE))
        send(grp.at[r], grp.at[r], SEM["group"], on_rep((r + i + 1) % LINE))

    times(LINE - 1, send_blocks)

    activated = (preact * gated).astype(BF)
    g_in = dot(agg, grad_pre, ((0,), (0,)))
    g_out = dot(activated, og, ((0,), (0,)))
    wsend[0:4] = g_in.reshape(4, 64, WIDE)
    wsend[4:8] = g_out.reshape(4, 64, WIDE)
    column_sums = jnp.sum(grad_pre.astype(F32), axis=0, keepdims=True)
    row = lax.broadcasted_iota(jnp.int32, (8, HALF), 0)
    bsend[...] = jnp.where(
        row == 0, column_sums[:, :HALF], jnp.where(row == 1, column_sums[:, HALF:], 0.0)
    )

    def send_weights(i):
        to = (r + i + 1) % LINE
        send(wsend.at[to], wrecv.at[r], SEM["w_rep"], on_rep(to))
        send(bsend, brecv.at[r], SEM["b_rep"], on_rep(to))

    times(LINE - 1, send_weights)
    wrecv[r] = wsend[r]
    brecv[r] = bsend[...]

    lane = lax.broadcasted_iota(jnp.int32, (ROWS, ROWS), 1)
    for c in range(EDGES // ROWS):
        col = dst_ref[:, c : c + 1]
        v_dst[c * ROWS : (c + 1) * ROWS, :] = jnp.where((col & 127) == lane, col >> 7, -1).astype(BF)
    sub = lax.broadcasted_iota(jnp.int32, (ROWS, 512), 0)
    for c in range(EDGES // 512):
        cut = src_ref[:, c * 512 : (c + 1) * 512]
        v_src[:, c * 512 : (c + 1) * 512] = jnp.where((cut & 127) == sub, cut >> 7, -1).astype(BF)

    def one_hot(codes, high):
        if not isinstance(high, int):
            high = high.astype(F32)
        return jnp.where(codes == jnp.asarray(high, F32).astype(BF), BF(1), BF(0))

    got(ia.at[0:7], SEM["idx_a"])
    got(ib.at[0:7], SEM["idx_b"])
    sub = lax.broadcasted_iota(jnp.int32, (ROWS, WIDE), 0)
    for asked, picks in ((ia, pt_a), (ib, pt_b)):
        parts = []
        for g in range(2):
            part = asked[4 * g]
            for i in range(1, 4):
                part = jnp.maximum(part, asked[4 * g + i])
            parts.append(part)
        both = jnp.concatenate(parts, axis=1)
        for i in range(LINE):
            picks[i] = jnp.where(sub == both[i : i + 1, :], 1.0, 0.0).astype(BF)

    got(blk_b.at[0:7], SEM["one_b"])

    def pick_b(i):
        rows = dot(pt_b[i], blk_b[i], ((0,), (0,))).astype(BF)
        stage_b[:, i] = rows.reshape(LINE, SLOT, HALF)

    times(LINE, pick_b)
    mir_b[z] = stage_b[z]
    got(blk_a.at[0:7], SEM["one_a"])

    def pick_a(i):
        rows = dot(pt_a[i], blk_a[i], ((0,), (0,))).astype(BF)
        stage_a[:, i] = rows.reshape(LINE, SLOT, HALF)

    times(LINE, pick_a)
    mir_a[:, y] = stage_a[y]
    for c, offsets in enumerate(FWD):
        for j in offsets:
            if j:
                to = (z + LINE - j) % LINE
                send(stage_b.at[to], mir_b.at[z], TWO_B + c, on_z(to))
            block = (z + j) % LINE

            def send_a(i, block=block, c=c):
                to = (y + offset(i)) % LINE
                send(stage_a.at[to, block], mir_a.at[block, y], TWO_A + c, on_y(to))

            times(LINE - 1, send_a)

    got(grp.at[0:7], SEM["group"])
    step = 512

    def gather_group(i):
        at = pl.ds(pl.multiple_of(i * step, step), step)
        codes = v_dst[at, :]
        hot = jnp.concatenate([one_hot(codes, h) for h in range(LINE)], axis=1)
        fetched[at, :] = dot(hot, grp[...].reshape(LINE * ROWS, WIDE)).astype(BF)

    times(EDGES // step, gather_group)

    got(wrecv.at[0:7], SEM["w_rep"])
    got(brecv.at[0:7], SEM["b_rep"])
    total = wrecv[0]
    bias_total = brecv[0]
    for i in range(1, LINE):
        total = total + wrecv[i]
        bias_total = bias_total + brecv[i]
    zsend[:, :, :WIDE] = total.reshape(LINE, 8, WIDE)
    zsend[:, :, WIDE:] = jnp.broadcast_to(bias_total[None], (LINE, 8, HALF))

    def send_z(i):
        to = (z + offset(i)) % LINE
        send(zsend.at[to], zrecv.at[z], SEM["w_z"], on_z(to))

    times(LINE - 1, send_z)
    zrecv[z] = zsend[z]

    def gather_mirrors(c):
        offsets = FWD[c]
        got(mir_b.at[0 : len([j for j in offsets if j])], TWO_B + c)
        got(mir_a.at[0 : len(offsets), 0:7], TWO_A + c)
        blocks = [(z + j) % LINE for j in offsets]
        for n, block in enumerate(blocks):
            wbuf[n * WIDE : (n + 1) * WIDE, :HALF] = mir_a[block].reshape(WIDE, HALF)
            wbuf[n * WIDE : (n + 1) * WIDE, HALF:] = mir_b[block].reshape(WIDE, HALF)
        depth = len(blocks) * WIDE
        highs = [8 + 2 * block + h for block in blocks for h in range(2)]

        def run(i):
            at = pl.ds(pl.multiple_of(i * step, step), step)
            codes = v_dst[at, :]
            hot = jnp.concatenate([one_hot(codes, h) for h in highs], axis=1)
            fetched[at, :] = fetched[at, :] + dot(hot, wbuf[:depth, :]).astype(BF)

        times(EDGES // step, run)

    gather_mirrors(0)

    got(zrecv.at[0:7], SEM["w_z"])
    total = zrecv[0]
    for i in range(1, LINE):
        total = total + zrecv[i]
    ysend[...] = total

    def send_y(i):
        send(ysend, yrecv.at[y], SEM["w_y"], on_y((y + offset(i)) % LINE))

    times(LINE - 1, send_y)
    yrecv[y] = total

    for c in range(1, len(FWD)):
        gather_mirrors(c)

    for offsets in BWD:
        blocks = [(z + j) % LINE for j in offsets]
        hot = jnp.concatenate(
            [one_hot(v_src[...], 8 + 2 * block + h) for block in blocks for h in range(2)], axis=0
        )
        sums = dot(hot, fetched[...]).astype(BF)
        for n, (j, block) in enumerate(zip(offsets, blocks)):
            part = sums[n * WIDE : (n + 1) * WIDE]
            out_a[block] = part[:, :HALF].reshape(LINE, SLOT, HALF)
            out_b[block] = part[:, HALF:].reshape(LINE, SLOT, HALF)
            if j:
                send(out_b.at[block], rb.at[z], SEM["back_b"], on_z(block))
            else:
                rb[z] = out_b[block]
            ra[y, block] = out_a[block, y]

            def send_back(i, block=block):
                to = (y + offset(i)) % LINE
                send(out_a.at[block, to], ra.at[y, block], SEM["back_a"], on_y(to))

            times(LINE - 1, send_back)

    got(yrecv.at[0:7], SEM["w_y"])
    total = yrecv[0]
    for i in range(1, LINE):
        total = total + yrecv[i]
    bsum_ref[...] = total[:, WIDE:]
    zg[z] = total[:, :WIDE]

    def send_zg(i):
        send(zg.at[z], zg.at[z], SEM["w_zg"], on_z((z + offset(i)) % LINE))

    times(LINE - 1, send_zg)

    for c in range(2):
        hot = jnp.concatenate([one_hot(v_src[...], 4 * c + h) for h in range(4)], axis=0)
        gout[4 * c : 4 * c + 4] = dot(hot, fetched[...]).astype(BF).reshape(4, ROWS, WIDE)

    def send_sums(i):
        to = (r + i + 1) % LINE
        send(gout.at[to], gin.at[r], SEM["gsum"], on_rep(to))

    times(LINE - 1, send_sums)
    gin[r] = gout[r]

    got(zg.at[0:7], SEM["w_zg"])
    wfull[r] = zg[...].reshape(64, WIDE)

    def send_full(i):
        send(wfull.at[r], wfull.at[r], SEM["w_repg"], on_rep((r + i + 1) % LINE))

    times(LINE - 1, send_full)

    got(rb.at[0:7], SEM["back_b"])

    def add_b(i):
        sums = dot(pt_b[i], rb[:, i].reshape(WIDE, HALF))
        last_src_b[i] = sums.astype(BF)

    times(LINE, add_b)
    fb[y] = last_src_b[y]

    def send_last_b(i):
        to = (y + offset(i)) % LINE
        send(last_src_b.at[to], fb.at[y], SEM["last_b"], on_y(to))

    times(LINE - 1, send_last_b)
    got(ra.at[0:7], SEM["back_a"])

    def add_a(i):
        sums = dot(pt_a[i], ra[:, i].reshape(WIDE, HALF))
        last_src_a[i] = sums.astype(BF)

    times(LINE, add_a)
    fa[z] = last_src_a[z]

    def send_last_a(i):
        to = (z + offset(i)) % LINE
        send(last_src_a.at[to], fa.at[z], SEM["last_a"], on_z(to))

    times(LINE - 1, send_last_a)

    nodes = (1.0 + sw_ref[0]) * ga_ref[...].astype(F32)
    got(gin.at[0:7], SEM["gsum"])
    for i in range(LINE):
        nodes = nodes + gin[i].astype(F32)
    got(wfull.at[0:7], SEM["w_repg"])
    weights_ref[...] = wfull[...].reshape(LINE * 64, WIDE)
    got(fb.at[0:7], SEM["last_b"])
    right = nodes[:, HALF:]
    for i in range(LINE):
        right = right + fb[i].astype(F32)
    nodes_ref[:, HALF:] = right
    got(fa.at[0:7], SEM["last_a"])
    left = nodes[:, :HALF]
    for i in range(LINE):
        left = left + fa[i].astype(F32)
    nodes_ref[:, :HALF] = left

    for view, name in (
        (ia, "idx_a"), (ib, "idx_b"), (blk_a, "one_a"), (blk_b, "one_b"), (grp, "group"), (wrecv, "w_rep"),
        (brecv, "b_rep"), (zrecv, "w_z"), (yrecv, "w_y"), (zg, "w_zg"), (wfull, "w_repg"), (ra, "back_a"),
        (rb, "back_b"), (gin, "gsum"), (fa, "last_a"), (fb, "last_b"),
    ):
        sent(view.at[0:7], SEM[name])
    for c, offsets in enumerate(FWD):
        sent(mir_b.at[0 : len([j for j in offsets if j])], TWO_B + c)
        sent(mir_a.at[0 : len(offsets), 0:7], TWO_A + c)


def body(agg_feats, out_grad, w_in, w_out, bias_in, self_weight, mirror_rows, edge_src, edge_dst):
    me = lax.axis_index("dom")
    r = lax.axis_index("rep")
    z, y = me // LINE, me % LINE
    rows = mirror_rows[0, 0] - r * ROWS
    rows = jnp.tile(rows, (1, 4)).reshape(LINE, LINE, ROWS)
    quarter = lax.broadcasted_iota(jnp.int32, (1, 1, ROWS), 2) // SLOT
    idx_a = jnp.where(quarter == y % 4, rows.swapaxes(0, 1), -1)
    idx_b = jnp.where(quarter == z % 4, rows, -1)
    dst = edge_dst.reshape(EDGES // ROWS, ROWS).T
    src = edge_src.reshape(1, EDGES)

    vmem = pl.BlockSpec(memory_space=pltpu.VMEM)
    smem = pl.BlockSpec(memory_space=pltpu.SMEM)
    V = pltpu.VMEM
    scratch = [
        V((ROWS, WIDE), BF),
        V((LINE, ROWS, WIDE), BF),
        V((LINE, ROWS, HALF), BF), V((LINE, ROWS, HALF), BF),
        V((LINE, LINE, ROWS), jnp.int32), V((LINE, LINE, ROWS), jnp.int32),
        V((LINE, ROWS, WIDE), BF), V((LINE, ROWS, WIDE), BF),
        V((LINE, LINE, SLOT, HALF), BF), V((LINE, LINE, SLOT, HALF), BF),
        V((LINE, LINE, SLOT, HALF), BF), V((LINE, LINE, SLOT, HALF), BF),
        V((EDGES, ROWS), BF), V((ROWS, EDGES), BF),
        V((max(map(len, FWD)) * WIDE, WIDE), BF),
        V((EDGES, WIDE), BF),
        V((LINE, LINE, SLOT, HALF), BF), V((LINE, LINE, SLOT, HALF), BF),
        V((LINE, LINE, SLOT, HALF), BF), V((LINE, LINE, SLOT, HALF), BF),
        V((LINE, ROWS, HALF), BF), V((LINE, ROWS, HALF), BF),
        V((LINE, ROWS, HALF), BF), V((LINE, ROWS, HALF), BF),
        V((LINE, ROWS, WIDE), BF), V((LINE, ROWS, WIDE), BF),
        V((LINE, 64, WIDE), F32), V((LINE, 64, WIDE), F32),
        V((8, HALF), F32), V((LINE, 8, HALF), F32),
        V((LINE, 8, WIDE + HALF), F32), V((LINE, 8, WIDE + HALF), F32),
        V((8, WIDE + HALF), F32), V((LINE, 8, WIDE + HALF), F32),
        V((LINE, 8, WIDE), F32),
        V((LINE, 64, WIDE), F32),
        pltpu.SemaphoreType.DMA((N_SEM,)),
        pltpu.SemaphoreType.DMA((N_SEM,)),
    ]
    nodes, weights, bsum = pl.pallas_call(
        kernel,
        out_shape=(
            jax.ShapeDtypeStruct((ROWS, WIDE), F32),
            jax.ShapeDtypeStruct((2 * WIDE, WIDE), F32),
            jax.ShapeDtypeStruct((8, HALF), F32),
        ),
        in_specs=[vmem] * 5 + [smem] + [vmem] * 4,
        out_specs=(vmem, vmem, vmem),
        scratch_shapes=scratch,
        compiler_params=pltpu.CompilerParams(
            collective_id=0, has_side_effects=True, vmem_limit_bytes=48 << 20
        ),
    )(
        agg_feats, out_grad, w_in, w_out, bias_in.reshape(1, WIDE), self_weight, idx_a, idx_b, dst, src
    )
    scale = float(64 * LINE * ROWS) ** -0.5
    weights = weights * scale
    return nodes, weights[:WIDE], weights[WIDE:], bsum[:2].reshape(WIDE) * scale


def solution(mesh):
    placed = (
        P(("dom", "rep"), None), P(("dom", "rep"), None), P(), P(), P(), P(),
        P("dom", "rep", None, None), P("dom", "rep", None), P("dom", "rep", None),
    )
    return jax.shard_map(
        body, mesh=mesh, in_specs=placed, out_specs=(P(("dom", "rep"), None), P(), P(), P()), check_vma=False
    )
```

```python
import functools

import jax
import jax.numpy as jnp
from jax import lax
from jax.experimental import pallas as pl
from jax.experimental.pallas import tpu as pltpu
from jax.sharding import PartitionSpec as P

MESH = pl.DeviceIdType.MESH
BF = jnp.bfloat16
F32 = jnp.float32

LINE = 8
ROWS = 128
SLOT = 32
HALF = 128
WIDE = 256
EDGES = 4096
ORDER = (0, 1, 7, 2, 6, 3, 5, 4)
FWD = ((0, 1), (7, 2), (6, 3), (5,), (4,))
BWD = ((1,), (7, 2), (6, 3), (5, 4, 0))

STAGES = (
    "idx_a", "idx_b", "group", "w_rep", "b_rep", "w_z", "w_y", "w_zg", "w_repg",
    "back_a", "back_b", "gsum", "last_a", "last_b",
)
SEM = {name: i for i, name in enumerate(STAGES)}
TWO_A = len(STAGES)
TWO_B = TWO_A + len(FWD)
ONE_A = TWO_B + len(FWD)
ONE_B = ONE_A + LINE
N_SEM = ONE_B + LINE


def each(step):
    for j in ORDER[1:]:
        step(j)


def dot(a, b, dims=((1,), (0,))):
    return lax.dot_general(a, b, (dims, ((), ())), preferred_element_type=F32)


def kernel(
    agg_ref, og_ref, w_in_ref, w_out_ref, bias_ref, sw_ref, idx_a_ref, idx_b_ref, dst_ref, src_ref,
    nodes_ref, weights_ref, bsum_ref,
    ga_ref, grp, blk_a, blk_b, ia, ib, pt_a, pt_b, pc_a, pc_b, stage_a, stage_b, mir_a, mir_b,
    v_dst, v_src, fetched, out_a, out_b, ra, rb, last_src_a, last_src_b, fa, fb, gout, gin,
    wsend, wrecv, bsend, brecv, zsend, zrecv, ysend, yrecv, zg, wfull, ssem, rsem,
):
    me = lax.axis_index("dom")
    r = lax.axis_index("rep")
    z, y = me // LINE, me % LINE
    z_at, y_at, r_at = ([lax.rem(own + j, LINE) for j in range(LINE)] for own in (z, y, r))

    def on_z(to):
        return (to * LINE + y, r)

    def on_y(to):
        return (z * LINE + to, r)

    def on_rep(to):
        return (me, to)

    def send(src, dst, sem, device):
        pltpu.make_async_remote_copy(
            src_ref=src, dst_ref=dst, send_sem=ssem.at[sem], recv_sem=rsem.at[sem],
            device_id=device, device_id_type=MESH,
        ).start()

    def got(view, sem):
        pltpu.make_async_copy(view, view, rsem.at[sem]).wait()

    def sent(view, sem):
        pltpu.make_async_copy(view, view, ssem.at[sem]).wait()

    barrier = pltpu.get_barrier_semaphore()

    def greet(j):
        for device in (on_z(z_at[j]), on_y(y_at[j]), on_rep(r_at[j])):
            pl.semaphore_signal(barrier, inc=1, device_id=device, device_id_type=MESH)

    each(greet)

    agg, og = agg_ref[...], og_ref[...]
    preact = dot(agg, w_in_ref[...]) + bias_ref[...]
    gated = jax.nn.sigmoid(preact)
    back_act = dot(og, w_out_ref[...], ((1,), (1,)))
    grad_pre = (back_act * gated * (1.0 + preact * (1.0 - gated))).astype(BF)
    grad_agg = dot(grad_pre, w_in_ref[...], ((1,), (1,))).astype(BF)
    ga_ref[...] = grad_agg
    grp[r] = grad_agg
    blk_a[z] = grad_agg[:, :HALF]
    blk_b[y] = grad_agg[:, HALF:]
    ia[y] = idx_a_ref[y]
    ib[z] = idx_b_ref[z]

    pl.semaphore_wait(barrier, 3 * (LINE - 1))

    def send_idx(j):
        to = y_at[j]
        send(idx_a_ref.at[to], ia.at[y], SEM["idx_a"], on_y(to))
        to = z_at[j]
        send(idx_b_ref.at[to], ib.at[z], SEM["idx_b"], on_z(to))

    each(send_idx)

    def send_blocks(j):
        send(blk_a.at[z], blk_a.at[z], ONE_A + LINE - j, on_z(z_at[j]))
        send(blk_b.at[y], blk_b.at[y], ONE_B + LINE - j, on_y(y_at[j]))

    each(send_blocks)

    activated = (preact * gated).astype(BF)
    g_in = dot(agg, grad_pre, ((0,), (0,)))
    g_out = dot(activated, og, ((0,), (0,)))
    wsend[0:4] = g_in.astype(BF).reshape(4, 64, WIDE)
    wsend[4:8] = g_out.astype(BF).reshape(4, 64, WIDE)
    column_sums = jnp.sum(grad_pre.astype(F32), axis=0, keepdims=True)
    row = lax.broadcasted_iota(jnp.int32, (8, HALF), 0)
    bsend[...] = jnp.where(
        row == 0, column_sums[:, :HALF], jnp.where(row == 1, column_sums[:, HALF:], 0.0)
    )

    def send_weights(j):
        to = r_at[j]
        send(wsend.at[to], wrecv.at[r], SEM["w_rep"], on_rep(to))
        send(bsend, brecv.at[r], SEM["b_rep"], on_rep(to))

    each(send_weights)

    def send_group(j):
        send(grp.at[r], grp.at[r], SEM["group"], on_rep(r_at[j]))

    each(send_group)
    wrecv[r] = wsend[r]
    brecv[r] = bsend[...]

    got(ia.at[0:7], SEM["idx_a"])
    got(ib.at[0:7], SEM["idx_b"])
    sub = lax.broadcasted_iota(jnp.int32, (ROWS, WIDE), 0)
    lane = lax.broadcasted_iota(jnp.int32, (WIDE, ROWS), 1)
    for came, picks, columns in ((ia, pt_a, pc_a), (ib, pt_b, pc_b)):
        parts = []
        for g in range(2):
            part = came[4 * g]
            for i in range(1, 4):
                part = jnp.maximum(part, came[4 * g + i])
            parts.append(part)
        both = jnp.concatenate(parts, axis=1)
        for i in range(LINE):
            picks[i] = jnp.where(sub == both[i : i + 1, :], 1.0, 0.0).astype(BF)
        both = both.T
        for i in range(LINE):
            columns[i] = jnp.where(lane == both[:, i : i + 1], 1.0, 0.0).astype(BF)

    chunk_of = {j: c for c, offsets in enumerate(FWD) for j in offsets}
    for j in ORDER:
        block = z_at[j]
        if j:
            got(blk_a.at[0], ONE_A + j)
        rows = dot(pc_a[block], blk_a[block]).astype(BF)
        stage_a[:, block] = rows.reshape(LINE, SLOT, HALF)

        def send_a(j, block=block, c=chunk_of[j]):
            to = y_at[j]
            send(stage_a.at[to, block], mir_a.at[block, y], TWO_A + c, on_y(to))

        each(send_a)
        block = y_at[j]
        if j:
            got(blk_b.at[0], ONE_B + j)
        rows = dot(pc_b[block], blk_b[block]).astype(BF)
        stage_b[:, block] = rows.reshape(LINE, SLOT, HALF)
    got(wrecv.at[0:7], SEM["w_rep"])
    got(brecv.at[0:7], SEM["b_rep"])
    total = wrecv[0].astype(F32)
    bias_total = brecv[0]
    for i in range(1, LINE):
        total = total + wrecv[i].astype(F32)
        bias_total = bias_total + brecv[i]
    zsend[:, :, :WIDE] = total.reshape(LINE, 8, WIDE)
    zsend[:, :, WIDE:] = jnp.broadcast_to(bias_total[None], (LINE, 8, HALF))

    def send_z(j):
        to = z_at[j]
        send(zsend.at[to], zrecv.at[z], SEM["w_z"], on_z(to))

    each(send_z)
    zrecv[z] = zsend[z]

    for j in ORDER[1:]:
        to = z_at[LINE - j]
        send(stage_b.at[to], mir_b.at[z], TWO_B + chunk_of[j], on_z(to))
    mir_b[z] = stage_b[z]
    mir_a[:, y] = stage_a[y]

    lane = lax.broadcasted_iota(jnp.int32, (ROWS, ROWS), 1)
    for c in range(EDGES // ROWS):
        col = dst_ref[:, c : c + 1]
        v_dst[c * ROWS : (c + 1) * ROWS, :] = jnp.where((col & 127) == lane, col >> 7, -1).astype(BF)
    sub = lax.broadcasted_iota(jnp.int32, (ROWS, 512), 0)
    for c in range(EDGES // 512):
        cut = src_ref[:, c * 512 : (c + 1) * 512]
        v_src[:, c * 512 : (c + 1) * 512] = jnp.where((cut & 127) == sub, cut >> 7, -1).astype(BF)

    def one_hot(codes, high):
        if not isinstance(high, int):
            high = high.astype(F32)
        return jnp.where(codes == jnp.asarray(high, F32).astype(BF), BF(1), BF(0))

    got(grp.at[0:7], SEM["group"])
    hot = jnp.concatenate([one_hot(v_dst[...], h) for h in range(LINE)], axis=1)
    fetched[...] = dot(hot, grp[...].reshape(LINE * ROWS, WIDE)).astype(BF)

    got(zrecv.at[0:7], SEM["w_z"])
    total = zrecv[0]
    for i in range(1, LINE):
        total = total + zrecv[i]
    ysend[...] = total

    def send_y(j):
        send(ysend, yrecv.at[y], SEM["w_y"], on_y(y_at[j]))

    each(send_y)
    yrecv[y] = total

    def gather_mirrors(c):
        offsets = FWD[c]
        got(mir_b.at[0 : len([j for j in offsets if j])], TWO_B + c)
        got(mir_a.at[0 : len(offsets), 0:7], TWO_A + c)
        blocks = [z_at[j] for j in offsets]
        values = jnp.concatenate(
            [
                jnp.concatenate([mir_a[block].reshape(WIDE, HALF), mir_b[block].reshape(WIDE, HALF)], axis=1)
                for block in blocks
            ],
            axis=0,
        )
        hot = jnp.concatenate(
            [one_hot(v_dst[...], 8 + 2 * block + h) for block in blocks for h in range(2)], axis=1
        )
        fetched[...] = fetched[...] + dot(hot, values).astype(BF)

    for c in range(len(FWD)):
        gather_mirrors(c)

    got(yrecv.at[0:7], SEM["w_y"])
    total = yrecv[0]
    for i in range(1, LINE):
        total = total + yrecv[i]
    bsum_ref[...] = total[:, WIDE:]
    zg[z] = total[:, :WIDE]

    def send_zg(j):
        send(zg.at[z], zg.at[z], SEM["w_zg"], on_z(z_at[j]))

    each(send_zg)

    for c, offsets in enumerate(BWD):
        blocks = [z_at[j] for j in offsets]
        hot = jnp.concatenate(
            [one_hot(v_src[...], 8 + 2 * block + h) for block in blocks for h in range(2)], axis=0
        )
        sums = dot(hot, fetched[...]).astype(BF)
        for n, (j, block) in enumerate(zip(offsets, blocks)):
            part = sums[n * WIDE : (n + 1) * WIDE]
            out_a[block] = part[:, :HALF].reshape(LINE, SLOT, HALF)
            out_b[block] = part[:, HALF:].reshape(LINE, SLOT, HALF)
            if j:
                send(out_b.at[block], rb.at[z], SEM["back_b"], on_z(block))
            else:
                rb[z] = out_b[block]
            ra[y, block] = out_a[block, y]

            def send_back(j, block=block):
                to = y_at[j]
                send(out_a.at[block, to], ra.at[y, block], SEM["back_a"], on_y(to))

            each(send_back)
        if c != 1:
            continue

        got(zg.at[0:7], SEM["w_zg"])
        wfull[r] = zg[...].reshape(64, WIDE)

        def send_full(j):
            send(wfull.at[r], wfull.at[r], SEM["w_repg"], on_rep(r_at[j]))

        each(send_full)

    for c in range(2):
        hot = jnp.concatenate([one_hot(v_src[...], 4 * c + h) for h in range(4)], axis=0)
        gout[4 * c : 4 * c + 4] = dot(hot, fetched[...]).astype(BF).reshape(4, ROWS, WIDE)

    def send_sums(j):
        to = r_at[j]
        send(gout.at[to], gin.at[r], SEM["gsum"], on_rep(to))

    each(send_sums)
    gin[r] = gout[r]

    got(rb.at[0:7], SEM["back_b"])

    for i in range(LINE):
        sums = dot(pt_b[i], rb[:, i].reshape(WIDE, HALF))
        last_src_b[i] = sums.astype(BF)
    fb[y] = last_src_b[y]

    def send_last_b(j):
        to = y_at[j]
        send(last_src_b.at[to], fb.at[y], SEM["last_b"], on_y(to))

    each(send_last_b)
    got(ra.at[0:7], SEM["back_a"])

    for i in range(LINE):
        sums = dot(pt_a[i], ra[:, i].reshape(WIDE, HALF))
        last_src_a[i] = sums.astype(BF)
    fa[z] = last_src_a[z]

    def send_last_a(j):
        to = z_at[j]
        send(last_src_a.at[to], fa.at[z], SEM["last_a"], on_z(to))

    each(send_last_a)

    nodes = (1.0 + sw_ref[0]) * ga_ref[...].astype(F32)
    got(gin.at[0:7], SEM["gsum"])
    for i in range(LINE):
        nodes = nodes + gin[i].astype(F32)
    got(wfull.at[0:7], SEM["w_repg"])
    weights_ref[...] = wfull[...].reshape(LINE * 64, WIDE)
    got(fb.at[0:7], SEM["last_b"])
    right = nodes[:, HALF:]
    for i in range(LINE):
        right = right + fb[i].astype(F32)
    nodes_ref[:, HALF:] = right
    got(fa.at[0:7], SEM["last_a"])
    left = nodes[:, :HALF]
    for i in range(LINE):
        left = left + fa[i].astype(F32)
    nodes_ref[:, :HALF] = left

    for view, name in (
        (ia, "idx_a"), (ib, "idx_b"), (grp, "group"), (wrecv, "w_rep"),
        (brecv, "b_rep"), (zrecv, "w_z"), (yrecv, "w_y"), (zg, "w_zg"), (wfull, "w_repg"), (ra, "back_a"),
        (rb, "back_b"), (gin, "gsum"), (fa, "last_a"), (fb, "last_b"),
    ):
        sent(view.at[0:7], SEM[name])
    for j in range(1, LINE):
        sent(blk_a.at[0], ONE_A + j)
        sent(blk_b.at[0], ONE_B + j)
    for c, offsets in enumerate(FWD):
        sent(mir_b.at[0 : len([j for j in offsets if j])], TWO_B + c)
        sent(mir_a.at[0 : len(offsets), 0:7], TWO_A + c)


def body(agg_feats, out_grad, w_in, w_out, bias_in, self_weight, mirror_rows, edge_src, edge_dst):
    me = lax.axis_index("dom")
    r = lax.axis_index("rep")
    z, y = me // LINE, me % LINE
    rows = mirror_rows[0, 0] - r * ROWS
    rows = jnp.tile(rows, (1, 4)).reshape(LINE, LINE, ROWS)
    quarter = lax.broadcasted_iota(jnp.int32, (1, 1, ROWS), 2) // SLOT
    idx_a = jnp.where(quarter == y % 4, rows.swapaxes(0, 1), -1)
    idx_b = jnp.where(quarter == z % 4, rows, -1)
    dst = edge_dst.reshape(EDGES // ROWS, ROWS).T
    src = edge_src.reshape(1, EDGES)

    vmem = pl.BlockSpec(memory_space=pltpu.VMEM)
    smem = pl.BlockSpec(memory_space=pltpu.SMEM)
    V = pltpu.VMEM
    scratch = [
        V((ROWS, WIDE), BF),
        V((LINE, ROWS, WIDE), BF),
        V((LINE, ROWS, HALF), BF), V((LINE, ROWS, HALF), BF),
        V((LINE, LINE, ROWS), jnp.int32), V((LINE, LINE, ROWS), jnp.int32),
        V((LINE, ROWS, WIDE), BF), V((LINE, ROWS, WIDE), BF),
        V((LINE, WIDE, ROWS), BF), V((LINE, WIDE, ROWS), BF),
        V((LINE, LINE, SLOT, HALF), BF), V((LINE, LINE, SLOT, HALF), BF),
        V((LINE, LINE, SLOT, HALF), BF), V((LINE, LINE, SLOT, HALF), BF),
        V((EDGES, ROWS), BF), V((ROWS, EDGES), BF),
        V((EDGES, WIDE), BF),
        V((LINE, LINE, SLOT, HALF), BF), V((LINE, LINE, SLOT, HALF), BF),
        V((LINE, LINE, SLOT, HALF), BF), V((LINE, LINE, SLOT, HALF), BF),
        V((LINE, ROWS, HALF), BF), V((LINE, ROWS, HALF), BF),
        V((LINE, ROWS, HALF), BF), V((LINE, ROWS, HALF), BF),
        V((LINE, ROWS, WIDE), BF), V((LINE, ROWS, WIDE), BF),
        V((LINE, 64, WIDE), BF), V((LINE, 64, WIDE), BF),
        V((8, HALF), F32), V((LINE, 8, HALF), F32),
        V((LINE, 8, WIDE + HALF), F32), V((LINE, 8, WIDE + HALF), F32),
        V((8, WIDE + HALF), F32), V((LINE, 8, WIDE + HALF), F32),
        V((LINE, 8, WIDE), F32),
        V((LINE, 64, WIDE), F32),
        pltpu.SemaphoreType.DMA((N_SEM,)),
        pltpu.SemaphoreType.DMA((N_SEM,)),
    ]
    nodes, weights, bsum = pl.pallas_call(
        kernel,
        out_shape=(
            jax.ShapeDtypeStruct((ROWS, WIDE), F32),
            jax.ShapeDtypeStruct((2 * WIDE, WIDE), F32),
            jax.ShapeDtypeStruct((8, HALF), F32),
        ),
        in_specs=[vmem] * 5 + [smem] + [vmem] * 4,
        out_specs=(vmem, vmem, vmem),
        scratch_shapes=scratch,
        compiler_params=pltpu.CompilerParams(
            collective_id=0, has_side_effects=True, vmem_limit_bytes=48 << 20
        ),
    )(
        agg_feats, out_grad, w_in, w_out, bias_in.reshape(1, WIDE), self_weight, idx_a, idx_b, dst, src
    )
    scale = float(64 * LINE * ROWS) ** -0.5
    weights = weights * scale
    return nodes, weights[:WIDE], weights[WIDE:], bsum[:2].reshape(WIDE) * scale


def solution(mesh):
    placed = (
        P(("dom", "rep"), None), P(("dom", "rep"), None), P(), P(), P(), P(),
        P("dom", "rep", None, None), P("dom", "rep", None), P("dom", "rep", None),
    )
    return jax.shard_map(
        body, mesh=mesh, in_specs=placed, out_specs=(P(("dom", "rep"), None), P(), P(), P()), check_vma=False
    )
```

```python
import functools

import jax
import jax.numpy as jnp
from jax import lax
from jax.experimental import pallas as pl
from jax.experimental.pallas import tpu as pltpu
from jax.sharding import PartitionSpec as P

MESH = pl.DeviceIdType.MESH
BF = jnp.bfloat16
F32 = jnp.float32

LINE = 8
ROWS = 128
SLOT = 32
HALF = 128
WIDE = 256
EDGES = 4096
ORDER = (0, 1, 7, 2, 6, 3, 5, 4)
FWD = ((0, 1), (7, 2), (6, 3), (5,), (4,))
BWD = ((1,), (7, 2), (6, 3), (5, 4, 0))

STAGES = (
    "idx_a", "idx_b", "group", "w_rep", "b_rep", "w_z", "w_y", "w_zg", "w_repg",
    "back_a", "back_b", "gsum", "last_a", "last_b",
)
SEM = {name: i for i, name in enumerate(STAGES)}
TWO_A = len(STAGES)
TWO_B = TWO_A + len(FWD)
ONE_A = TWO_B + len(FWD)
ONE_B = ONE_A + LINE
N_SEM = ONE_B + LINE


def each(step):
    for j in ORDER[1:]:
        step(j)


def dot(a, b, dims=((1,), (0,))):
    return lax.dot_general(a, b, (dims, ((), ())), preferred_element_type=F32)


def kernel(
    agg_ref, og_ref, w_in_ref, w_out_ref, bias_ref, sw_ref, idx_a_ref, idx_b_ref, dst_ref, src_ref,
    nodes_ref, weights_ref, bsum_ref,
    ga_ref, grp, blk_a, blk_b, ia, ib, pt_a, pt_b, pc_a, pc_b, stage_a, stage_b, mir_a, mir_b,
    v_dst, v_src, fetched, out_a, out_b, ra, rb, last_src_a, last_src_b, fa, fb, gout, gin,
    wsend, wrecv, bsend, brecv, zsend, zrecv, ysend, yrecv, zg, wfull, ssem, rsem,
):
    me = lax.axis_index("dom")
    r = lax.axis_index("rep")
    z, y = me // LINE, me % LINE
    z_at, y_at, r_at = ([lax.rem(own + j, LINE) for j in range(LINE)] for own in (z, y, r))

    def on_z(to):
        return (to * LINE + y, r)

    def on_y(to):
        return (z * LINE + to, r)

    def on_rep(to):
        return (me, to)

    def send(src, dst, sem, device):
        pltpu.make_async_remote_copy(
            src_ref=src, dst_ref=dst, send_sem=ssem.at[sem], recv_sem=rsem.at[sem],
            device_id=device, device_id_type=MESH,
        ).start()

    def got(view, sem):
        pltpu.make_async_copy(view, view, rsem.at[sem]).wait()

    def sent(view, sem):
        pltpu.make_async_copy(view, view, ssem.at[sem]).wait()

    barrier = pltpu.get_barrier_semaphore()

    def greet(j):
        for device in (on_z(z_at[j]), on_y(y_at[j]), on_rep(r_at[j])):
            pl.semaphore_signal(barrier, inc=1, device_id=device, device_id_type=MESH)

    each(greet)

    agg, og = agg_ref[...], og_ref[...]
    preact = dot(agg, w_in_ref[...]) + bias_ref[...]
    gated = jax.nn.sigmoid(preact)
    back_act = dot(og, w_out_ref[...], ((1,), (1,)))
    grad_pre = (back_act * gated * (1.0 + preact * (1.0 - gated))).astype(BF)
    grad_agg = dot(grad_pre, w_in_ref[...], ((1,), (1,))).astype(BF)
    ga_ref[...] = grad_agg
    grp[r] = grad_agg
    blk_a[z] = grad_agg[:, :HALF]
    blk_b[y] = grad_agg[:, HALF:]
    ia[y] = idx_a_ref[y]
    ib[z] = idx_b_ref[z]

    pl.semaphore_wait(barrier, 3 * (LINE - 1))

    def send_idx(j):
        to = y_at[j]
        send(idx_a_ref.at[to], ia.at[y], SEM["idx_a"], on_y(to))
        to = z_at[j]
        send(idx_b_ref.at[to], ib.at[z], SEM["idx_b"], on_z(to))

    each(send_idx)

    def send_blocks(j):
        send(blk_a.at[z], blk_a.at[z], ONE_A + LINE - j, on_z(z_at[j]))
        send(blk_b.at[y], blk_b.at[y], ONE_B + LINE - j, on_y(y_at[j]))

    each(send_blocks)

    activated = (preact * gated).astype(BF)
    g_in = dot(agg, grad_pre, ((0,), (0,)))
    g_out = dot(activated, og, ((0,), (0,)))
    wsend[0:4] = g_in.astype(BF).reshape(4, 64, WIDE)
    wsend[4:8] = g_out.astype(BF).reshape(4, 64, WIDE)
    column_sums = jnp.sum(grad_pre.astype(F32), axis=0, keepdims=True)
    row = lax.broadcasted_iota(jnp.int32, (8, HALF), 0)
    bsend[...] = jnp.where(
        row == 0, column_sums[:, :HALF], jnp.where(row == 1, column_sums[:, HALF:], 0.0)
    )

    def send_weights(j):
        to = r_at[j]
        send(wsend.at[to], wrecv.at[r], SEM["w_rep"], on_rep(to))
        send(bsend, brecv.at[r], SEM["b_rep"], on_rep(to))

    each(send_weights)

    def send_group(j):
        send(grp.at[r], grp.at[r], SEM["group"], on_rep(r_at[j]))

    each(send_group)
    wrecv[r] = wsend[r]
    brecv[r] = bsend[...]

    got(ia.at[0:7], SEM["idx_a"])
    got(ib.at[0:7], SEM["idx_b"])
    sub = lax.broadcasted_iota(jnp.int32, (ROWS, WIDE), 0)
    lane = lax.broadcasted_iota(jnp.int32, (WIDE, ROWS), 1)
    for came, picks, columns in ((ia, pt_a, pc_a), (ib, pt_b, pc_b)):
        parts = []
        for g in range(2):
            part = came[4 * g]
            for i in range(1, 4):
                part = jnp.maximum(part, came[4 * g + i])
            parts.append(part)
        both = jnp.concatenate(parts, axis=1)
        for i in range(LINE):
            picks[i] = jnp.where(sub == both[i : i + 1, :], 1.0, 0.0).astype(BF)
        both = both.T
        for i in range(LINE):
            columns[i] = jnp.where(lane == both[:, i : i + 1], 1.0, 0.0).astype(BF)

    chunk_of = {j: c for c, offsets in enumerate(FWD) for j in offsets}
    for j in ORDER:
        block = z_at[j]
        if j:
            got(blk_a.at[0], ONE_A + j)
        rows = dot(pc_a[block], blk_a[block]).astype(BF)
        stage_a[:, block] = rows.reshape(LINE, SLOT, HALF)

        def send_a(j, block=block, c=chunk_of[j]):
            to = y_at[j]
            send(stage_a.at[to, block], mir_a.at[block, y], TWO_A + c, on_y(to))

        each(send_a)
        block = y_at[j]
        if j:
            got(blk_b.at[0], ONE_B + j)
        rows = dot(pc_b[block], blk_b[block]).astype(BF)
        stage_b[:, block] = rows.reshape(LINE, SLOT, HALF)
        if j != 5:
            continue

        got(wrecv.at[0:7], SEM["w_rep"])
        got(brecv.at[0:7], SEM["b_rep"])
        total = wrecv[0].astype(F32)
        bias_total = brecv[0]
        for i in range(1, LINE):
            total = total + wrecv[i].astype(F32)
            bias_total = bias_total + brecv[i]
        zsend[:, :, :WIDE] = total.reshape(LINE, 8, WIDE)
        zsend[:, :, WIDE:] = jnp.broadcast_to(bias_total[None], (LINE, 8, HALF))

        def send_z(j):
            to = z_at[j]
            send(zsend.at[to], zrecv.at[z], SEM["w_z"], on_z(to))

        each(send_z)
        zrecv[z] = zsend[z]

    for j in ORDER[1:]:
        to = z_at[LINE - j]
        send(stage_b.at[to], mir_b.at[z], TWO_B + chunk_of[j], on_z(to))
    mir_b[z] = stage_b[z]
    mir_a[:, y] = stage_a[y]

    lane = lax.broadcasted_iota(jnp.int32, (ROWS, ROWS), 1)
    targets = dst_ref[...].T
    for c in range(EDGES // ROWS):
        col = targets[:, c : c + 1]
        v_dst[c * ROWS : (c + 1) * ROWS, :] = jnp.where((col & 127) == lane, col >> 7, -1).astype(BF)
    sub = lax.broadcasted_iota(jnp.int32, (ROWS, 512), 0)
    for c in range(EDGES // 512):
        cut = src_ref[:, c * 512 : (c + 1) * 512]
        v_src[:, c * 512 : (c + 1) * 512] = jnp.where((cut & 127) == sub, cut >> 7, -1).astype(BF)

    def one_hot(codes, high):
        if not isinstance(high, int):
            high = high.astype(F32)
        return jnp.where(codes == jnp.asarray(high, F32).astype(BF), BF(1), BF(0))

    got(grp.at[0:7], SEM["group"])
    hot = jnp.concatenate([one_hot(v_dst[...], h) for h in range(LINE)], axis=1)
    fetched[...] = dot(hot, grp[...].reshape(LINE * ROWS, WIDE)).astype(BF)

    def gather_mirrors(c):
        offsets = FWD[c]
        got(mir_b.at[0 : len([j for j in offsets if j])], TWO_B + c)
        got(mir_a.at[0 : len(offsets), 0:7], TWO_A + c)
        blocks = [z_at[j] for j in offsets]
        values = jnp.concatenate(
            [
                jnp.concatenate([mir_a[block].reshape(WIDE, HALF), mir_b[block].reshape(WIDE, HALF)], axis=1)
                for block in blocks
            ],
            axis=0,
        )
        hot = jnp.concatenate(
            [one_hot(v_dst[...], 8 + 2 * block + h) for block in blocks for h in range(2)], axis=1
        )
        fetched[...] = fetched[...] + dot(hot, values).astype(BF)

    gather_mirrors(0)

    got(zrecv.at[0:7], SEM["w_z"])
    total = zrecv[0]
    for i in range(1, LINE):
        total = total + zrecv[i]
    ysend[...] = total

    def send_y(j):
        send(ysend, yrecv.at[y], SEM["w_y"], on_y(y_at[j]))

    each(send_y)
    yrecv[y] = total

    for c in range(1, len(FWD)):
        gather_mirrors(c)

    got(yrecv.at[0:7], SEM["w_y"])
    total = yrecv[0]
    for i in range(1, LINE):
        total = total + yrecv[i]
    bsum_ref[...] = total[:, WIDE:]
    zg[z] = total[:, :WIDE]

    def send_zg(j):
        send(zg.at[z], zg.at[z], SEM["w_zg"], on_z(z_at[j]))

    each(send_zg)

    for c, offsets in enumerate(BWD):
        blocks = [z_at[j] for j in offsets]
        hot = jnp.concatenate(
            [one_hot(v_src[...], 8 + 2 * block + h) for block in blocks for h in range(2)], axis=0
        )
        sums = dot(hot, fetched[...]).astype(BF)
        for n, (j, block) in enumerate(zip(offsets, blocks)):
            part = sums[n * WIDE : (n + 1) * WIDE]
            out_a[block] = part[:, :HALF].reshape(LINE, SLOT, HALF)
            out_b[block] = part[:, HALF:].reshape(LINE, SLOT, HALF)
            if j:
                send(out_b.at[block], rb.at[z], SEM["back_b"], on_z(block))
            else:
                rb[z] = out_b[block]
            ra[y, block] = out_a[block, y]

            def send_back(j, block=block):
                to = y_at[j]
                send(out_a.at[block, to], ra.at[y, block], SEM["back_a"], on_y(to))

            each(send_back)
        if c != 3:
            continue

        got(zg.at[0:7], SEM["w_zg"])
        wfull[r] = zg[...].reshape(64, WIDE)

        def send_full(j):
            send(wfull.at[r], wfull.at[r], SEM["w_repg"], on_rep(r_at[j]))

        each(send_full)

    for c in range(2):
        hot = jnp.concatenate([one_hot(v_src[...], 4 * c + h) for h in range(4)], axis=0)
        gout[4 * c : 4 * c + 4] = dot(hot, fetched[...]).astype(BF).reshape(4, ROWS, WIDE)

    def send_sums(j):
        to = r_at[j]
        send(gout.at[to], gin.at[r], SEM["gsum"], on_rep(to))

    each(send_sums)
    gin[r] = gout[r]

    got(rb.at[0:7], SEM["back_b"])

    for i in range(LINE):
        sums = dot(pt_b[i], rb[:, i].reshape(WIDE, HALF))
        last_src_b[i] = sums.astype(BF)
    fb[y] = last_src_b[y]

    def send_last_b(j):
        to = y_at[j]
        send(last_src_b.at[to], fb.at[y], SEM["last_b"], on_y(to))

    each(send_last_b)
    got(ra.at[0:7], SEM["back_a"])

    for i in range(LINE):
        sums = dot(pt_a[i], ra[:, i].reshape(WIDE, HALF))
        last_src_a[i] = sums.astype(BF)
    fa[z] = last_src_a[z]

    def send_last_a(j):
        to = z_at[j]
        send(last_src_a.at[to], fa.at[z], SEM["last_a"], on_z(to))

    each(send_last_a)

    nodes = (1.0 + sw_ref[0]) * ga_ref[...].astype(F32)
    got(gin.at[0:7], SEM["gsum"])
    for i in range(LINE):
        nodes = nodes + gin[i].astype(F32)
    got(wfull.at[0:7], SEM["w_repg"])
    weights_ref[...] = wfull[...].reshape(LINE * 64, WIDE)
    got(fb.at[0:7], SEM["last_b"])
    right = nodes[:, HALF:]
    for i in range(LINE):
        right = right + fb[i].astype(F32)
    nodes_ref[:, HALF:] = right
    got(fa.at[0:7], SEM["last_a"])
    left = nodes[:, :HALF]
    for i in range(LINE):
        left = left + fa[i].astype(F32)
    nodes_ref[:, :HALF] = left

    for view, name in (
        (ia, "idx_a"), (ib, "idx_b"), (grp, "group"), (wrecv, "w_rep"),
        (brecv, "b_rep"), (zrecv, "w_z"), (yrecv, "w_y"), (zg, "w_zg"), (wfull, "w_repg"), (ra, "back_a"),
        (rb, "back_b"), (gin, "gsum"), (fa, "last_a"), (fb, "last_b"),
    ):
        sent(view.at[0:7], SEM[name])
    for j in range(1, LINE):
        sent(blk_a.at[0], ONE_A + j)
        sent(blk_b.at[0], ONE_B + j)
    for c, offsets in enumerate(FWD):
        sent(mir_b.at[0 : len([j for j in offsets if j])], TWO_B + c)
        sent(mir_a.at[0 : len(offsets), 0:7], TWO_A + c)


def body(agg_feats, out_grad, w_in, w_out, bias_in, self_weight, mirror_rows, edge_src, edge_dst):
    me = lax.axis_index("dom")
    r = lax.axis_index("rep")
    z, y = me // LINE, me % LINE
    rows = mirror_rows[0, 0] - r * ROWS
    rows = jnp.tile(rows, (1, 4)).reshape(LINE, LINE, ROWS)
    quarter = lax.broadcasted_iota(jnp.int32, (1, 1, ROWS), 2) // SLOT
    idx_a = jnp.where(quarter == y % 4, rows.swapaxes(0, 1), -1)
    idx_b = jnp.where(quarter == z % 4, rows, -1)
    dst = edge_dst.reshape(EDGES // ROWS, ROWS)
    src = edge_src.reshape(1, EDGES)

    vmem = pl.BlockSpec(memory_space=pltpu.VMEM)
    smem = pl.BlockSpec(memory_space=pltpu.SMEM)
    V = pltpu.VMEM
    scratch = [
        V((ROWS, WIDE), BF),
        V((LINE, ROWS, WIDE), BF),
        V((LINE, ROWS, HALF), BF), V((LINE, ROWS, HALF), BF),
        V((LINE, LINE, ROWS), jnp.int32), V((LINE, LINE, ROWS), jnp.int32),
        V((LINE, ROWS, WIDE), BF), V((LINE, ROWS, WIDE), BF),
        V((LINE, WIDE, ROWS), BF), V((LINE, WIDE, ROWS), BF),
        V((LINE, LINE, SLOT, HALF), BF), V((LINE, LINE, SLOT, HALF), BF),
        V((LINE, LINE, SLOT, HALF), BF), V((LINE, LINE, SLOT, HALF), BF),
        V((EDGES, ROWS), BF), V((ROWS, EDGES), BF),
        V((EDGES, WIDE), BF),
        V((LINE, LINE, SLOT, HALF), BF), V((LINE, LINE, SLOT, HALF), BF),
        V((LINE, LINE, SLOT, HALF), BF), V((LINE, LINE, SLOT, HALF), BF),
        V((LINE, ROWS, HALF), BF), V((LINE, ROWS, HALF), BF),
        V((LINE, ROWS, HALF), BF), V((LINE, ROWS, HALF), BF),
        V((LINE, ROWS, WIDE), BF), V((LINE, ROWS, WIDE), BF),
        V((LINE, 64, WIDE), BF), V((LINE, 64, WIDE), BF),
        V((8, HALF), F32), V((LINE, 8, HALF), F32),
        V((LINE, 8, WIDE + HALF), F32), V((LINE, 8, WIDE + HALF), F32),
        V((8, WIDE + HALF), F32), V((LINE, 8, WIDE + HALF), F32),
        V((LINE, 8, WIDE), F32),
        V((LINE, 64, WIDE), F32),
        pltpu.SemaphoreType.DMA((N_SEM,)),
        pltpu.SemaphoreType.DMA((N_SEM,)),
    ]
    nodes, weights, bsum = pl.pallas_call(
        kernel,
        out_shape=(
            jax.ShapeDtypeStruct((ROWS, WIDE), F32),
            jax.ShapeDtypeStruct((2 * WIDE, WIDE), F32),
            jax.ShapeDtypeStruct((8, HALF), F32),
        ),
        in_specs=[vmem] * 5 + [smem] + [vmem] * 4,
        out_specs=(vmem, vmem, vmem),
        scratch_shapes=scratch,
        compiler_params=pltpu.CompilerParams(
            collective_id=0, has_side_effects=True, vmem_limit_bytes=48 << 20
        ),
    )(
        agg_feats, out_grad, w_in, w_out, bias_in.reshape(1, WIDE), self_weight, idx_a, idx_b, dst, src
    )
    scale = float(64 * LINE * ROWS) ** -0.5
    weights = weights * scale
    return nodes, weights[:WIDE], weights[WIDE:], bsum[:2].reshape(WIDE) * scale


def solution(mesh):
    placed = (
        P(("dom", "rep"), None), P(("dom", "rep"), None), P(), P(), P(), P(),
        P("dom", "rep", None, None), P("dom", "rep", None), P("dom", "rep", None),
    )
    return jax.shard_map(
        body, mesh=mesh, in_specs=placed, out_specs=(P(("dom", "rep"), None), P(), P(), P()), check_vma=False
    )
```

```python
import functools

import jax
import jax.numpy as jnp
from jax import lax
from jax.experimental import pallas as pl
from jax.experimental.pallas import tpu as pltpu
from jax.sharding import PartitionSpec as P

MESH = pl.DeviceIdType.MESH
BF = jnp.bfloat16
F32 = jnp.float32

LINE = 8
ROWS = 128
SLOT = 32
HALF = 128
WIDE = 256
EDGES = 4096
ORDER = (0, 1, 7, 2, 6, 3, 5, 4)
FWD = ((0, 1), (7, 2), (6, 3), (5,), (4,))
BWD = ((1, 7), (2, 6), (3, 5), (4, 0))

STAGES = (
    "idx_a", "idx_b", "group", "w_rep", "b_rep", "w_z", "w_y", "w_zg", "w_repg",
    "back_a", "back_b", "gsum", "last_a", "last_b",
)
SEM = {name: i for i, name in enumerate(STAGES)}
TWO_A = len(STAGES)
TWO_B = TWO_A + len(FWD)
ONE_A = TWO_B + len(FWD)
ONE_B = ONE_A + LINE
N_SEM = ONE_B + LINE


def each(step):
    for j in ORDER[1:]:
        step(j)


def dot(a, b, dims=((1,), (0,))):
    return lax.dot_general(a, b, (dims, ((), ())), preferred_element_type=F32)


def kernel(
    agg_ref, og_ref, w_in_ref, w_out_ref, bias_ref, sw_ref, idx_a_ref, idx_b_ref, dst_ref, src_ref,
    nodes_ref, weights_ref, bsum_ref,
    ga_ref, grp, blk_a, blk_b, ia, ib, pt_a, pt_b, pc_a, pc_b, stage_a, stage_b, mir_a, mir_b,
    v_dst, v_src, fetched, out_a, out_b, ra, rb, last_src_a, last_src_b, fa, fb, gout, gin,
    wsend, wrecv, bsend, brecv, zsend, zrecv, ysend, yrecv, zg, wfull, ssem, rsem,
):
    me = lax.axis_index("dom")
    r = lax.axis_index("rep")
    z, y = me // LINE, me % LINE
    z_at, y_at, r_at = ([lax.rem(own + j, LINE) for j in range(LINE)] for own in (z, y, r))

    def on_z(to):
        return (to * LINE + y, r)

    def on_y(to):
        return (z * LINE + to, r)

    def on_rep(to):
        return (me, to)

    def send(src, dst, sem, device):
        pltpu.make_async_remote_copy(
            src_ref=src, dst_ref=dst, send_sem=ssem.at[sem], recv_sem=rsem.at[sem],
            device_id=device, device_id_type=MESH,
        ).start()

    def got(view, sem):
        pltpu.make_async_copy(view, view, rsem.at[sem]).wait()

    def sent(view, sem):
        pltpu.make_async_copy(view, view, ssem.at[sem]).wait()

    barrier = pltpu.get_barrier_semaphore()

    def greet(j):
        for device in (on_z(z_at[j]), on_y(y_at[j]), on_rep(r_at[j])):
            pl.semaphore_signal(barrier, inc=1, device_id=device, device_id_type=MESH)

    each(greet)

    agg, og = agg_ref[...], og_ref[...]
    preact = dot(agg, w_in_ref[...]) + bias_ref[...]
    gated = jax.nn.sigmoid(preact)
    back_act = dot(og, w_out_ref[...], ((1,), (1,)))
    grad_pre = (back_act * gated * (1.0 + preact * (1.0 - gated))).astype(BF)
    grad_agg = dot(grad_pre, w_in_ref[...], ((1,), (1,))).astype(BF)
    ga_ref[...] = grad_agg
    grp[r] = grad_agg
    blk_a[z] = grad_agg[:, :HALF]
    blk_b[y] = grad_agg[:, HALF:]
    ia[y] = idx_a_ref[y]
    ib[z] = idx_b_ref[z]

    pl.semaphore_wait(barrier, 3 * (LINE - 1))

    def send_idx(j):
        to = y_at[j]
        send(idx_a_ref.at[to], ia.at[y], SEM["idx_a"], on_y(to))
        to = z_at[j]
        send(idx_b_ref.at[to], ib.at[z], SEM["idx_b"], on_z(to))

    each(send_idx)

    def send_blocks(j):
        send(blk_a.at[z], blk_a.at[z], ONE_A + LINE - j, on_z(z_at[j]))
        send(blk_b.at[y], blk_b.at[y], ONE_B + LINE - j, on_y(y_at[j]))

    each(send_blocks)

    activated = (preact * gated).astype(BF)
    g_in = dot(agg, grad_pre, ((0,), (0,)))
    g_out = dot(activated, og, ((0,), (0,)))
    wsend[0:4] = g_in.astype(BF).reshape(4, 64, WIDE)
    wsend[4:8] = g_out.astype(BF).reshape(4, 64, WIDE)
    column_sums = jnp.sum(grad_pre.astype(F32), axis=0, keepdims=True)
    row = lax.broadcasted_iota(jnp.int32, (8, HALF), 0)
    bsend[...] = jnp.where(
        row == 0, column_sums[:, :HALF], jnp.where(row == 1, column_sums[:, HALF:], 0.0)
    )

    def send_weights(j):
        to = r_at[j]
        send(wsend.at[to], wrecv.at[r], SEM["w_rep"], on_rep(to))
        send(bsend, brecv.at[r], SEM["b_rep"], on_rep(to))

    each(send_weights)

    def send_group(j):
        send(grp.at[r], grp.at[r], SEM["group"], on_rep(r_at[j]))

    each(send_group)
    wrecv[r] = wsend[r]
    brecv[r] = bsend[...]

    got(ia.at[0:7], SEM["idx_a"])
    got(ib.at[0:7], SEM["idx_b"])
    sub = lax.broadcasted_iota(jnp.int32, (ROWS, WIDE), 0)
    lane = lax.broadcasted_iota(jnp.int32, (WIDE, ROWS), 1)
    for came, picks, columns in ((ia, pt_a, pc_a), (ib, pt_b, pc_b)):
        parts = []
        for g in range(2):
            part = came[4 * g]
            for i in range(1, 4):
                part = jnp.maximum(part, came[4 * g + i])
            parts.append(part)
        both = jnp.concatenate(parts, axis=1)
        for i in range(LINE):
            picks[i] = jnp.where(sub == both[i : i + 1, :], 1.0, 0.0).astype(BF)
        both = both.T
        for i in range(LINE):
            columns[i] = jnp.where(lane == both[:, i : i + 1], 1.0, 0.0).astype(BF)

    chunk_of = {j: c for c, offsets in enumerate(FWD) for j in offsets}
    for j in ORDER:
        block = z_at[j]
        if j:
            got(blk_a.at[0], ONE_A + j)
        rows = dot(pc_a[block], blk_a[block]).astype(BF)
        stage_a[:, block] = rows.reshape(LINE, SLOT, HALF)

        def send_a(j, block=block, c=chunk_of[j]):
            to = y_at[j]
            send(stage_a.at[to, block], mir_a.at[block, y], TWO_A + c, on_y(to))

        each(send_a)
        block = y_at[j]
        if j:
            got(blk_b.at[0], ONE_B + j)
        rows = dot(pc_b[block], blk_b[block]).astype(BF)
        stage_b[:, block] = rows.reshape(LINE, SLOT, HALF)
        if j != 5:
            continue

        got(wrecv.at[0:7], SEM["w_rep"])
        got(brecv.at[0:7], SEM["b_rep"])
        total = wrecv[0].astype(F32)
        bias_total = brecv[0]
        for i in range(1, LINE):
            total = total + wrecv[i].astype(F32)
            bias_total = bias_total + brecv[i]
        zsend[:, :, :WIDE] = total.reshape(LINE, 8, WIDE)
        zsend[:, :, WIDE:] = jnp.broadcast_to(bias_total[None], (LINE, 8, HALF))

        def send_z(j):
            to = z_at[j]
            send(zsend.at[to], zrecv.at[z], SEM["w_z"], on_z(to))

        each(send_z)
        zrecv[z] = zsend[z]

    for j in ORDER[1:]:
        to = z_at[LINE - j]
        send(stage_b.at[to], mir_b.at[z], TWO_B + chunk_of[j], on_z(to))
    mir_b[z] = stage_b[z]
    mir_a[:, y] = stage_a[y]

    lane = lax.broadcasted_iota(jnp.int32, (ROWS, ROWS), 1)
    targets = dst_ref[...].T
    for c in range(EDGES // ROWS):
        col = targets[:, c : c + 1]
        v_dst[c * ROWS : (c + 1) * ROWS, :] = jnp.where((col & 127) == lane, col >> 7, -1).astype(BF)
    sub = lax.broadcasted_iota(jnp.int32, (ROWS, 512), 0)
    for c in range(EDGES // 512):
        cut = src_ref[:, c * 512 : (c + 1) * 512]
        v_src[:, c * 512 : (c + 1) * 512] = jnp.where((cut & 127) == sub, cut >> 7, -1).astype(BF)

    def one_hot(codes, high):
        if not isinstance(high, int):
            high = high.astype(F32)
        return jnp.where(codes == jnp.asarray(high, F32).astype(BF), BF(1), BF(0))

    got(grp.at[0:7], SEM["group"])
    hot = jnp.concatenate([one_hot(v_dst[...], h) for h in range(LINE)], axis=1)
    fetched[...] = dot(hot, grp[...].reshape(LINE * ROWS, WIDE)).astype(BF)

    def gather_mirrors(c):
        offsets = FWD[c]
        got(mir_b.at[0 : len([j for j in offsets if j])], TWO_B + c)
        got(mir_a.at[0 : len(offsets), 0:7], TWO_A + c)
        blocks = [z_at[j] for j in offsets]
        values = jnp.concatenate(
            [
                jnp.concatenate([mir_a[block].reshape(WIDE, HALF), mir_b[block].reshape(WIDE, HALF)], axis=1)
                for block in blocks
            ],
            axis=0,
        )
        hot = jnp.concatenate(
            [one_hot(v_dst[...], 8 + 2 * block + h) for block in blocks for h in range(2)], axis=1
        )
        fetched[...] = fetched[...] + dot(hot, values).astype(BF)

    gather_mirrors(0)

    got(zrecv.at[0:7], SEM["w_z"])
    total = zrecv[0]
    for i in range(1, LINE):
        total = total + zrecv[i]
    ysend[...] = total

    def send_y(j):
        send(ysend, yrecv.at[y], SEM["w_y"], on_y(y_at[j]))

    each(send_y)
    yrecv[y] = total

    for c in range(1, len(FWD)):
        gather_mirrors(c)

    got(yrecv.at[0:7], SEM["w_y"])
    total = yrecv[0]
    for i in range(1, LINE):
        total = total + yrecv[i]
    bsum_ref[...] = total[:, WIDE:]
    zg[z] = total[:, :WIDE]

    def send_zg(j):
        send(zg.at[z], zg.at[z], SEM["w_zg"], on_z(z_at[j]))

    each(send_zg)

    for c, offsets in enumerate(BWD):
        blocks = [z_at[j] for j in offsets]
        hot = jnp.concatenate(
            [one_hot(v_src[...], 8 + 2 * block + h) for block in blocks for h in range(2)], axis=0
        )
        sums = dot(hot, fetched[...]).astype(BF)
        for n, (j, block) in enumerate(zip(offsets, blocks)):
            part = sums[n * WIDE : (n + 1) * WIDE]
            out_a[block] = part[:, :HALF].reshape(LINE, SLOT, HALF)
            out_b[block] = part[:, HALF:].reshape(LINE, SLOT, HALF)
            if j:
                send(out_b.at[block], rb.at[z], SEM["back_b"], on_z(block))
            else:
                rb[z] = out_b[block]
            ra[y, block] = out_a[block, y]

            def send_back(j, block=block):
                to = y_at[j]
                send(out_a.at[block, to], ra.at[y, block], SEM["back_a"], on_y(to))

            each(send_back)
        if c != 3:
            continue

        got(zg.at[0:7], SEM["w_zg"])
        wfull[r] = zg[...].reshape(64, WIDE)

        def send_full(j):
            send(wfull.at[r], wfull.at[r], SEM["w_repg"], on_rep(r_at[j]))

        each(send_full)

    for c in range(2):
        hot = jnp.concatenate([one_hot(v_src[...], 4 * c + h) for h in range(4)], axis=0)
        gout[4 * c : 4 * c + 4] = dot(hot, fetched[...]).astype(BF).reshape(4, ROWS, WIDE)

    def send_sums(j):
        to = r_at[j]
        send(gout.at[to], gin.at[r], SEM["gsum"], on_rep(to))

    each(send_sums)
    gin[r] = gout[r]

    got(rb.at[0:7], SEM["back_b"])

    for i in range(LINE):
        sums = dot(pt_b[i], rb[:, i].reshape(WIDE, HALF))
        last_src_b[i] = sums.astype(BF)
    fb[y] = last_src_b[y]

    def send_last_b(j):
        to = y_at[j]
        send(last_src_b.at[to], fb.at[y], SEM["last_b"], on_y(to))

    each(send_last_b)
    got(ra.at[0:7], SEM["back_a"])

    for i in range(LINE):
        sums = dot(pt_a[i], ra[:, i].reshape(WIDE, HALF))
        last_src_a[i] = sums.astype(BF)
    fa[z] = last_src_a[z]

    def send_last_a(j):
        to = z_at[j]
        send(last_src_a.at[to], fa.at[z], SEM["last_a"], on_z(to))

    each(send_last_a)

    nodes = (1.0 + sw_ref[0]) * ga_ref[...].astype(F32)
    got(gin.at[0:7], SEM["gsum"])
    for i in range(LINE):
        nodes = nodes + gin[i].astype(F32)
    got(wfull.at[0:7], SEM["w_repg"])
    weights_ref[...] = wfull[...].reshape(LINE * 64, WIDE)
    got(fb.at[0:7], SEM["last_b"])
    right = nodes[:, HALF:]
    for i in range(LINE):
        right = right + fb[i].astype(F32)
    nodes_ref[:, HALF:] = right
    got(fa.at[0:7], SEM["last_a"])
    left = nodes[:, :HALF]
    for i in range(LINE):
        left = left + fa[i].astype(F32)
    nodes_ref[:, :HALF] = left

    for view, name in (
        (ia, "idx_a"), (ib, "idx_b"), (grp, "group"), (wrecv, "w_rep"),
        (brecv, "b_rep"), (zrecv, "w_z"), (yrecv, "w_y"), (zg, "w_zg"), (wfull, "w_repg"), (ra, "back_a"),
        (rb, "back_b"), (gin, "gsum"), (fa, "last_a"), (fb, "last_b"),
    ):
        sent(view.at[0:7], SEM[name])
    for j in range(1, LINE):
        sent(blk_a.at[0], ONE_A + j)
        sent(blk_b.at[0], ONE_B + j)
    for c, offsets in enumerate(FWD):
        sent(mir_b.at[0 : len([j for j in offsets if j])], TWO_B + c)
        sent(mir_a.at[0 : len(offsets), 0:7], TWO_A + c)


def body(agg_feats, out_grad, w_in, w_out, bias_in, self_weight, mirror_rows, edge_src, edge_dst):
    me = lax.axis_index("dom")
    r = lax.axis_index("rep")
    z, y = me // LINE, me % LINE
    rows = mirror_rows[0, 0] - r * ROWS
    rows = jnp.tile(rows, (1, 4)).reshape(LINE, LINE, ROWS)
    quarter = lax.broadcasted_iota(jnp.int32, (1, 1, ROWS), 2) // SLOT
    idx_a = jnp.where(quarter == y % 4, rows.swapaxes(0, 1), -1)
    idx_b = jnp.where(quarter == z % 4, rows, -1)
    dst = edge_dst.reshape(EDGES // ROWS, ROWS)
    src = edge_src.reshape(1, EDGES)

    vmem = pl.BlockSpec(memory_space=pltpu.VMEM)
    smem = pl.BlockSpec(memory_space=pltpu.SMEM)
    V = pltpu.VMEM
    scratch = [
        V((ROWS, WIDE), BF),
        V((LINE, ROWS, WIDE), BF),
        V((LINE, ROWS, HALF), BF), V((LINE, ROWS, HALF), BF),
        V((LINE, LINE, ROWS), jnp.int32), V((LINE, LINE, ROWS), jnp.int32),
        V((LINE, ROWS, WIDE), BF), V((LINE, ROWS, WIDE), BF),
        V((LINE, WIDE, ROWS), BF), V((LINE, WIDE, ROWS), BF),
        V((LINE, LINE, SLOT, HALF), BF), V((LINE, LINE, SLOT, HALF), BF),
        V((LINE, LINE, SLOT, HALF), BF), V((LINE, LINE, SLOT, HALF), BF),
        V((EDGES, ROWS), BF), V((ROWS, EDGES), BF),
        V((EDGES, WIDE), BF),
        V((LINE, LINE, SLOT, HALF), BF), V((LINE, LINE, SLOT, HALF), BF),
        V((LINE, LINE, SLOT, HALF), BF), V((LINE, LINE, SLOT, HALF), BF),
        V((LINE, ROWS, HALF), BF), V((LINE, ROWS, HALF), BF),
        V((LINE, ROWS, HALF), BF), V((LINE, ROWS, HALF), BF),
        V((LINE, ROWS, WIDE), BF), V((LINE, ROWS, WIDE), BF),
        V((LINE, 64, WIDE), BF), V((LINE, 64, WIDE), BF),
        V((8, HALF), F32), V((LINE, 8, HALF), F32),
        V((LINE, 8, WIDE + HALF), F32), V((LINE, 8, WIDE + HALF), F32),
        V((8, WIDE + HALF), F32), V((LINE, 8, WIDE + HALF), F32),
        V((LINE, 8, WIDE), F32),
        V((LINE, 64, WIDE), F32),
        pltpu.SemaphoreType.DMA((N_SEM,)),
        pltpu.SemaphoreType.DMA((N_SEM,)),
    ]
    nodes, weights, bsum = pl.pallas_call(
        kernel,
        out_shape=(
            jax.ShapeDtypeStruct((ROWS, WIDE), F32),
            jax.ShapeDtypeStruct((2 * WIDE, WIDE), F32),
            jax.ShapeDtypeStruct((8, HALF), F32),
        ),
        in_specs=[vmem] * 5 + [smem] + [vmem] * 4,
        out_specs=(vmem, vmem, vmem),
        scratch_shapes=scratch,
        compiler_params=pltpu.CompilerParams(
            collective_id=0, has_side_effects=True, vmem_limit_bytes=48 << 20
        ),
    )(
        agg_feats, out_grad, w_in, w_out, bias_in.reshape(1, WIDE), self_weight, idx_a, idx_b, dst, src
    )
    scale = float(64 * LINE * ROWS) ** -0.5
    weights = weights * scale
    return nodes, weights[:WIDE], weights[WIDE:], bsum[:2].reshape(WIDE) * scale


def solution(mesh):
    placed = (
        P(("dom", "rep"), None), P(("dom", "rep"), None), P(), P(), P(), P(),
        P("dom", "rep", None, None), P("dom", "rep", None), P("dom", "rep", None),
    )
    return jax.shard_map(
        body, mesh=mesh, in_specs=placed, out_specs=(P(("dom", "rep"), None), P(), P(), P()), check_vma=False
    )
```
